256 devices in a mesh: dp: 8 (over z_hi, core), seq: 32 (over x, y, z_lo).
Axes of the slice: x: 4, y: 4, z: 8 (z_hi: 4, z_lo: 2; z = z_hi * 2 + z_lo), core: 2. Of those that a mesh axis runs over, the one named last changes fastest.
Arguments:
- queries: bfloat16 [8, 8192, 1024], P('dp', 'seq'), may hold values from -6 to 6
- image_feats: bfloat16 [8, 32, 64, 8192], P('dp', 'seq'), may hold values from -6 to 6
- key_weight: bfloat16 [8192, 128], replicated, may hold values from -0.0625 to 0.0625
- value_weight: bfloat16 [8192, 128], replicated, may hold values from -0.0625 to 0.0625
- image_pos: int32 [8, 32], P('dp'), may hold values from 0 to 8191, as said below
- image_slot: int32 [8, 32], P('dp'), may hold values from 0 to 31, each once within a row
- ctx_grad: bfloat16 [8, 8192, 1024], P('dp', 'seq'), may hold values from -24 to 24
Outputs:
- context: bfloat16 [8, 8192, 1024], P('dp', 'seq')
- query_grad: bfloat16 [8, 8192, 1024], P('dp', 'seq')
- feats_grad: bfloat16 [8, 32, 64, 8192], P('dp', 'seq')
- key_wgrad: float32 [8192, 128], P('seq')
- value_wgrad: float32 [8192, 128], P('seq')
The draws below stay inside these ranges and needn't reach their ends.
Inputs may be any that keep to these rules, and one draw needn't show every extreme that they name: `image_pos`: for each document the positions rise strictly, the first is 0 and the last is 8191. Each document's row is a permutation: image i is stored in slot image_slot[i], held by seq index image_slot[i].
All inputs are finite; a program needn't handle non-finite values.
Results may differ from the reference program's by a relative error of at most 0.0075.
Values may be sent and summed in bfloat16 or wider, within the bound.
A program may use at most 128 MiB of HBM per device.

```python
import jax
import jax.numpy as jnp
from jax import lax

D = 8192
HD = 128
GROUP = 8
VT = 64
IMAGES = 32
TOKENS = 8192
DOCS = 8


def draw_image_pos(key, part):
    key = jax.random.fold_in(key, 11)
    doc_keys = jax.random.split(key, DOCS)

    def one_document(doc_key):
        picks = jax.random.permutation(doc_key, TOKENS - 2)[:IMAGES - 2] + 1
        picks = jnp.sort(picks.astype(jnp.int32))
        first = jnp.zeros((1,), jnp.int32)
        last = jnp.full((1,), TOKENS - 1, jnp.int32)
        return jnp.concatenate([first, picks, last]).astype(jnp.int32)
    return jax.vmap(one_document)(doc_keys)


def raised(drawn, stream_key, source, target, parts, factor):
    def block_of(dim):
        return (jnp.arange(drawn.shape[dim]) // (drawn.shape[dim] // parts)).reshape((-1,) + (1,) * (drawn.ndim - 1 - dim))

    near = jax.random.permutation(stream_key, parts)[block_of(target)]
    second = (block_of(target) + parts // 2) % parts
    return jnp.where((block_of(source) == near) | (block_of(source) == second), factor * drawn, drawn)


def block_levels(rng, shape, cuts, low, top_value):
    gain, own = 1.0, jax.random.fold_in(rng, 6)
    for axis_at, blocks in cuts:
        steps = jnp.exp(jax.random.uniform(jax.random.fold_in(own, axis_at), (blocks,), jnp.float32, low / len(cuts), top_value / len(cuts)))
        gain = gain * jnp.repeat(steps, shape[axis_at] // blocks).reshape([-1 if axis == axis_at else 1 for axis in range(len(shape))])
    return gain


def noise(own_key, dims, width, reach, shards=(), kind=jnp.bfloat16):
    loudness = block_levels(own_key, dims, shards, -0.22, 0.18) if shards else 1.0
    values = jax.random.normal(own_key, dims, jnp.float32) * width * loudness
    return jnp.minimum(jnp.maximum(values, -reach), reach).astype(kind)


def gaussian_with(key, dims, deviation, limit, cuts, heavy, kind=jnp.bfloat16):
    result = deviation * jax.random.normal(key, dims, jnp.float32)
    if cuts:
        result = result * block_levels(key, dims, cuts, -0.22, 0.18)
    return jnp.clip(raised(result, jax.random.fold_in(key, 3), *heavy), -limit, limit).astype(kind)


def setup_inputs(seed: int = 0) -> dict:
    key_list = jax.random.split(jax.random.key(seed), 8)
    queries = noise(key_list[0], (DOCS, TOKENS, GROUP * HD), 1.0, 6.0, ((0, 8), (1, 32)))
    image_feats = gaussian_with(key_list[1], (DOCS, IMAGES, VT, D), 1.0, 6.0, ((0, 8), (1, 32)), (1, 3, 32, 2.75))
    key_weight = noise(key_list[2], (D, HD), D ** -0.5, 0.0625)
    value_weight = noise(key_list[3], (D, HD), D ** -0.5, 0.0625)
    image_pos = draw_image_pos(jax.random.fold_in(key_list[7], 71), 0)
    image_slot = jax.vmap(lambda own: jax.random.permutation(own, IMAGES))(jax.random.split(key_list[5], DOCS)).reshape((DOCS, IMAGES)).astype(jnp.int32)
    ctx_grad = noise(key_list[6], (DOCS, TOKENS, GROUP * HD), 4.0, 24.0, ((0, 8), (1, 32)))
    return {"queries": queries, "image_feats": image_feats, "key_weight": key_weight, "value_weight": value_weight, "image_pos": image_pos, "image_slot": image_slot, "ctx_grad": ctx_grad}


NORM_EPS = 1e-05

def norm_rows(inputs):
    return inputs * lax.rsqrt(lax.optimization_barrier(jnp.mean(inputs * inputs, axis=-1, keepdims=True)) + NORM_EPS)

def norm_back(inputs, upstream):
    factor = lax.rsqrt(lax.optimization_barrier(jnp.mean(inputs * inputs, axis=-1, keepdims=True)) + NORM_EPS)
    normed = inputs * factor
    return factor * (upstream - normed * lax.optimization_barrier(jnp.mean(upstream * normed, axis=-1, keepdims=True)))

def slot_positions(image_pos, image_slot):
    image_count = image_slot.shape[0]
    matches = image_slot[:, None] == jnp.arange(image_count, dtype=jnp.int32)[None, :]
    return lax.optimization_barrier(jnp.sum(jnp.where(matches, image_pos[:, None], 0), axis=0)).astype(jnp.int32)

def attend_block(query_block, ctx_block, tok_pos, key_table, value_table, key_pos, score_scale):
    across = (((1,), (1,)), ((), ()))
    stacked = (((0,), (0,)), ((), ()))
    scores = lax.dot_general(query_block, key_table, across, preferred_element_type=jnp.float32) * score_scale
    visible = key_pos[None, :] <= tok_pos[:, None]
    exp_scores = jnp.where(visible, jnp.exp(scores), jnp.zeros_like(scores))
    soft_weights = exp_scores / lax.optimization_barrier(jnp.sum(exp_scores, axis=1, keepdims=True))
    soft_round = soft_weights.astype(jnp.bfloat16)
    context = jnp.dot(soft_round, value_table, preferred_element_type=jnp.float32).astype(jnp.bfloat16)
    prob_grad = lax.dot_general(ctx_block, value_table, across, preferred_element_type=jnp.float32)
    centre = lax.optimization_barrier(jnp.sum(soft_weights * prob_grad, axis=1, keepdims=True))
    score_full = soft_weights * (prob_grad - centre) * score_scale
    score_grad = score_full.astype(jnp.bfloat16)
    query_grad = jnp.dot(score_grad, key_table, preferred_element_type=jnp.float32)
    key_part = lax.dot_general(score_full, query_block.astype(jnp.float32), stacked, precision=lax.Precision.HIGHEST, preferred_element_type=jnp.float32)
    value_part = lax.dot_general(soft_round, ctx_block, stacked, preferred_element_type=jnp.float32)
    return (context, query_grad, key_part, value_part)

def attend_all(normed, ctx_rows, tok_pos, key_table, value_table, key_pos, block_rows):
    total_rows, head_dim = normed.shape
    block_count = total_rows // block_rows
    score_scale = head_dim ** (-0.5)

    def scan_step(running, block_item):
        results = attend_block(block_item[0], block_item[1], block_item[2], key_table, value_table, key_pos, score_scale)
        return ((running[0] + results[2], running[1] + results[3]), (results[0], results[1]))
    zero_grad = jnp.zeros((key_table.shape[0], head_dim), jnp.float32)
    block_items = (normed.reshape(block_count, block_rows, head_dim), ctx_rows.reshape(block_count, block_rows, head_dim), tok_pos.reshape(block_count, block_rows))
    grad_sums, outputs = lax.scan(scan_step, (zero_grad, zero_grad), block_items)
    context = outputs[0].reshape(total_rows, head_dim)
    query_grad = outputs[1].reshape(total_rows, head_dim)
    return (context, query_grad, grad_sums[0], grad_sums[1])

def reference(queries, image_feats, key_weight, value_weight, image_pos, image_slot, ctx_grad):

    def one_document(document):
        query_doc, feats_doc, pos_doc, slot_doc, grad_doc = document
        feat_rows = feats_doc.reshape(IMAGES * VT, D)
        key_rows = jnp.dot(feat_rows, key_weight, preferred_element_type=jnp.float32)
        norm_keys = norm_rows(key_rows).astype(jnp.bfloat16)
        value_rows = jnp.dot(feat_rows, value_weight, preferred_element_type=jnp.float32).astype(jnp.bfloat16)
        key_pos = jnp.repeat(slot_positions(pos_doc, slot_doc), VT)
        query_raw = query_doc.reshape(TOKENS, GROUP, HD).astype(jnp.float32)
        normed = norm_rows(query_raw).astype(jnp.bfloat16).reshape(TOKENS * GROUP, HD)
        ctx_rows = grad_doc.reshape(TOKENS * GROUP, HD)
        tok_pos = (jnp.arange(TOKENS * GROUP, dtype=jnp.int32) // GROUP).astype(jnp.int32)
        block_rows = min(TOKENS * GROUP, 2048)
        context, normed_grad, key_grad, value_grad = attend_all(normed, ctx_rows, tok_pos, norm_keys, value_rows, key_pos, block_rows)
        query_grad = norm_back(query_raw, normed_grad.reshape(TOKENS, GROUP, HD)).astype(jnp.bfloat16)
        key_row_grad = norm_back(key_rows, key_grad).astype(jnp.bfloat16)
        value_round = value_grad.astype(jnp.bfloat16)
        feats_grad = jnp.dot(key_row_grad, key_weight.T, preferred_element_type=jnp.float32) + jnp.dot(value_round, value_weight.T, preferred_element_type=jnp.float32)
        feats_grad = feats_grad.astype(jnp.bfloat16).reshape(IMAGES, VT, D)
        key_wgrad = jnp.dot(feat_rows.T, key_row_grad, preferred_element_type=jnp.float32)
        value_wgrad = jnp.dot(feat_rows.T, value_round, preferred_element_type=jnp.float32)
        return (context.reshape(TOKENS, GROUP * HD), query_grad.reshape(TOKENS, GROUP * HD), feats_grad, key_wgrad, value_wgrad)
    results = lax.map(one_document, (queries, image_feats, image_pos, image_slot, ctx_grad))
    return (results[0], results[1], results[2], lax.optimization_barrier(jnp.sum(results[3], axis=0)), lax.optimization_barrier(jnp.sum(results[4], axis=0)))
```

```python
import functools

import jax
import jax.numpy as jnp
from jax import lax
from jax.experimental import pallas as pl
from jax.experimental.pallas import tpu as pltpu
from jax.sharding import PartitionSpec as P

NORM_EPS = 1e-05
LOG2E = 1.4426950408889634
HIDE = -30000.0
GROUP_DEVICES = 4
BF16 = jnp.bfloat16
F32 = jnp.float32
MESH = pl.DeviceIdType.MESH
ACROSS = (((1,), (1,)), ((), ()))


def dot(a, b):
    return jnp.dot(a, b, preferred_element_type=F32)


def dot_across(a, b):
    return lax.dot_general(a, b, ACROSS, preferred_element_type=F32)


def row_factor(rows):
    return lax.rsqrt(jnp.mean(rows * rows, axis=-1, keepdims=True) + NORM_EPS)


def norm_back(rows, upstream):
    factor = row_factor(rows)
    normed = rows * factor
    return factor * (upstream - normed * jnp.mean(upstream * normed, axis=-1, keepdims=True))


def kernel(
    ns,
    nd,
    q_hbm,
    f_hbm,
    wk_hbm,
    wv_hbm,
    pos_ref,
    slot_ref,
    c_hbm,
    ctx_hbm,
    qg_hbm,
    fg_hbm,
    kw_hbm,
    vw_hbm,
    q_s,
    c_s,
    f_s,
    w_s,
    key_s,
    kv_s,
    y_s,
    do_s,
    vt_s,
    kt_s,
    e_s,
    ot_s,
    ctx_s,
    qg_s,
    fg_s,
    fsl_s,
    sendv_s,
    sendk_s,
    rsv_s,
    rsk_s,
    gv_s,
    gk_s,
    dp1_s,
    dp1r_s,
    dp2_s,
    in_sem,
    out_sem,
    ag_send,
    ag_recv,
    xs,
    xr,
):
    tokens, width = q_s.shape
    hd = 128
    heads = width // hd
    vt, d = f_s.shape
    ds_cols = d // ns
    chunk = GROUP_DEVICES * vt
    ng = ns // GROUP_DEVICES
    keys = ns * vt
    scale = hd ** (-0.5)
    dp_rows = ds_cols // nd

    me = lax.axis_index("seq")
    doc = lax.axis_index("dp")
    my_group = lax.div(me, GROUP_DEVICES)
    my_place = lax.rem(me, GROUP_DEVICES)

    def peer(g, j):
        return lax.rem(my_group + g, ng) * GROUP_DEVICES + lax.rem(my_place + j, GROUP_DEVICES)

    def doc_peer(o):
        return lax.rem(doc + o, nd)

    def block(index, size):
        return pl.ds(pl.multiple_of(index * size, size), size)

    pairs = [(g, j) for g in range(ng) for j in range(GROUP_DEVICES) if (g, j) != (0, 0)]

    steps = 4
    depth = d // steps
    w_copies = []
    for k in range(steps):
        rows = pl.ds(k * depth, depth)
        w_copies.append(
            (
                pltpu.make_async_copy(f_hbm.at[:, rows], f_s.at[:, rows], in_sem.at[3 * k]),
                pltpu.make_async_copy(
                    wk_hbm.at[rows, :], w_s.at[rows, pl.ds(0, hd)], in_sem.at[3 * k + 1]
                ),
                pltpu.make_async_copy(
                    wv_hbm.at[rows, :], w_s.at[rows, pl.ds(hd, hd)], in_sem.at[3 * k + 2]
                ),
            )
        )
    q_copy = pltpu.make_async_copy(q_hbm, q_s, in_sem.at[3 * steps])
    c_copy = pltpu.make_async_copy(c_hbm, c_s, in_sem.at[3 * steps + 1])
    for copies in w_copies:
        for copy in copies:
            copy.start()
    q_copy.start()
    c_copy.start()

    barrier = pltpu.get_barrier_semaphore()
    for g, j in pairs:
        pl.semaphore_signal(barrier, inc=1, device_id={"seq": peer(g, j)}, device_id_type=MESH)
    for o in range(1, nd):
        pl.semaphore_signal(barrier, inc=1, device_id={"dp": doc_peer(o)}, device_id_type=MESH)

    rows_kv = jnp.zeros((vt, 2 * hd), F32)
    for k in range(steps):
        for copy in w_copies[k]:
            copy.wait()
        rows = pl.ds(k * depth, depth)
        rows_kv = rows_kv + dot(f_s[:, rows], w_s[rows, :])
    key_rows = rows_kv[:, :hd]
    key_s[...] = key_rows
    mine = block(me, vt)
    kv_s[mine, :] = jnp.concatenate(
        [(key_rows * row_factor(key_rows)).astype(BF16), rows_kv[:, hd:].astype(BF16)], axis=1
    )
    pl.semaphore_wait(barrier, ns - 1 + nd - 1)

    def send(src, dst, send_sem, recv_sem, target):
        pltpu.make_async_remote_copy(
            src_ref=src,
            dst_ref=dst,
            send_sem=send_sem,
            recv_sem=recv_sem,
            device_id=target,
            device_id_type=MESH,
        ).start()

    def take(ref, sem):
        pltpu.make_async_copy(ref, ref, sem).wait()

    for g, j in pairs:
        send(kv_s.at[mine, :], kv_s.at[mine, :], ag_send.at[0], ag_recv.at[g], {"seq": peer(g, j)})

    lane = lax.broadcasted_iota(jnp.int32, (tokens, hd), 1)
    tok = me * tokens + lax.broadcasted_iota(jnp.int32, (tokens, hd), 0)
    hidden = jnp.where(pos_ref[...] > tok, HIDE, 0.0).astype(BF16)
    q_copy.wait()
    for h in range(heads):
        raw = q_s[:, pl.ds(h * hd, hd)].astype(F32)
        rows = pl.ds(h * tokens, tokens)
        y_s[rows, pl.ds(0, hd)] = (raw * row_factor(raw)).astype(BF16)
        y_s[rows, pl.ds(hd, hd)] = hidden

    def first_pass(g, first):
        group = lax.rem(my_group - g + ng, ng)
        rows = block(group, chunk)
        pair = kv_s[rows, :]
        slot_of_key = group * GROUP_DEVICES + lax.div(
            lax.broadcasted_iota(jnp.int32, (chunk, hd), 0), vt
        )
        marks = (slot_ref[...] == slot_of_key).astype(F32).astype(BF16)
        key_aug = jnp.concatenate([pair[:, :hd], marks], axis=1)
        value_t = pair[:, hd:].astype(F32).T.astype(BF16)
        kt_s[:, rows] = pair[:, :hd].astype(F32).T.astype(BF16)
        value_aug = jnp.concatenate([value_t, jnp.ones((hd, chunk), BF16)], axis=0)
        for h in range(heads):
            head = pl.ds(h * tokens, tokens)
            scores = dot_across(key_aug, y_s[head, :])
            weights = jnp.exp2(scores * (scale * LOG2E)).astype(BF16)
            e_s[rows, head] = weights
            part = dot(value_aug, weights)
            if first:
                ot_s[h] = part
            else:
                ot_s[h] += part

    take(kv_s.at[pl.ds(0, chunk - vt), :], ag_recv.at[0])
    first_pass(0, True)

    def first_step(g, carry):
        take(kv_s.at[pl.ds(0, chunk), :], ag_recv.at[g])
        first_pass(g, False)
        return carry

    lax.fori_loop(1, ng, first_step, 0)

    for g, j in pairs:
        to = peer(g, j)
        send(f_s.at[:, block(to, ds_cols)], fsl_s.at[mine, :], xs.at[0], xr.at[0], {"seq": to})
    fsl_s[mine, :] = f_s[:, block(me, ds_cols)]

    c_copy.wait()
    for h in range(heads):
        cols = pl.ds(h * hd, hd)
        both = ot_s[h].T
        inverse = 1.0 / both[:, hd:]
        context = both[:, :hd] * inverse
        ctx_s[:, cols] = context.astype(BF16)
        scaled = (c_s[:, cols].astype(F32) * inverse).astype(BF16)
        centre = -jnp.sum(context * scaled.astype(F32), axis=1, keepdims=True)
        high = centre.astype(BF16).astype(F32)
        low = centre - high
        extra = jnp.where(lane == 0, high, jnp.where(lane == 1, low, 0.0)).astype(BF16)
        rows = pl.ds(h * tokens, tokens)
        do_s[rows, pl.ds(0, hd)] = scaled
        do_s[rows, pl.ds(hd, hd)] = extra
    ctx_copy = pltpu.make_async_copy(ctx_s, ctx_hbm, out_sem.at[0])
    ctx_copy.start()

    def send_group(src, dst, send_sem, recv_sem, group, first):
        for j in range(first, GROUP_DEVICES):
            to = group * GROUP_DEVICES + lax.rem(my_place + j, GROUP_DEVICES)
            send(src.at[block(to, vt), :], dst.at[mine, :], send_sem, recv_sem, {"seq": to})

    def value_part(group):
        rows = block(group, chunk)
        sendv_s[rows, :] = dot(e_s[rows, :], do_s[:, pl.ds(0, hd)]).astype(BF16)

    def value_step(g, carry):
        group = lax.rem(my_group + g, ng)
        value_part(group)
        send_group(sendv_s, rsv_s, xs.at[1], xr.at[1], group, 0)
        return carry

    lax.fori_loop(1, ng, value_step, 0)
    value_part(my_group)
    send_group(sendv_s, rsv_s, xs.at[1], xr.at[1], my_group, 1)
    rsv_s[mine, :] = sendv_s[mine, :]

    lane_of_key = lax.broadcasted_iota(jnp.int32, (chunk, hd), 1)
    ones_two = jnp.where(lane_of_key < 2, 1.0, 0.0).astype(BF16)

    def key_part(group):
        rows = block(group, chunk)
        value_aug = jnp.concatenate([kv_s[rows, pl.ds(hd, hd)], ones_two], axis=1)
        for h in range(heads):
            head = pl.ds(h * tokens, tokens)
            part = dot_across(value_aug, do_s[head, :])
            e_s[rows, head] = (e_s[rows, head].astype(F32) * part).astype(BF16)
        sendk_s[rows, :] = (dot(e_s[rows, :], y_s[:, pl.ds(0, hd)]) * scale).astype(BF16)

    def key_step(g, carry):
        group = lax.rem(my_group + g, ng)
        key_part(group)
        send_group(sendk_s, rsk_s, xs.at[2], xr.at[2], group, 0)
        return carry

    lax.fori_loop(1, ng, key_step, 0)
    key_part(my_group)
    send_group(sendk_s, rsk_s, xs.at[2], xr.at[2], my_group, 1)
    rsk_s[mine, :] = sendk_s[mine, :]

    most = (ns - 1) * vt

    def add_up(ref):
        total = ref[pl.ds(0, vt), :].astype(F32)
        for s in range(1, ns):
            total = total + ref[pl.ds(s * vt, vt), :].astype(F32)
        return total

    take(rsv_s.at[pl.ds(0, most), :], xr.at[1])
    gv_s[mine, :] = add_up(rsv_s).astype(BF16)
    for g, j in pairs:
        send(gv_s.at[mine, :], gv_s.at[mine, :], xs.at[3], xr.at[3], {"seq": peer(g, j)})

    for h in range(heads):
        cols = pl.ds(h * hd, hd)
        upstream = dot(kt_s[...], e_s[:, pl.ds(h * tokens, tokens)]).T * scale
        qg_s[:, cols] = norm_back(q_s[:, cols].astype(F32), upstream).astype(BF16)
    qg_copy = pltpu.make_async_copy(qg_s, qg_hbm, out_sem.at[1])
    qg_copy.start()

    take(rsk_s.at[pl.ds(0, most), :], xr.at[2])
    gk_s[mine, :] = norm_back(key_s[...], add_up(rsk_s)).astype(BF16)
    for g, j in pairs:
        send(gk_s.at[mine, :], gk_s.at[mine, :], xs.at[4], xr.at[4], {"seq": peer(g, j)})

    row_grads = jnp.concatenate([gk_s[mine, :], gv_s[mine, :]], axis=1)
    for k in range(steps):
        rows = pl.ds(k * depth, depth)
        fg_s[:, rows] = dot_across(row_grads, w_s[rows, :]).astype(BF16)
    fg_copy = pltpu.make_async_copy(fg_s, fg_hbm, out_sem.at[2])
    fg_copy.start()

    take(fsl_s.at[pl.ds(0, most), :], xr.at[0])
    feats_t = fsl_s[...].astype(F32).T.astype(BF16)

    def reduce_first(part, grads):
        dp1_s[part] = dot(feats_t, grads[...]).astype(BF16)
        for o in range(1, nd):
            to = doc_peer(o)
            send(
                dp1_s.at[part, block(to, dp_rows), :],
                dp1r_s.at[part, block(doc, dp_rows), :],
                xs.at[5 + part],
                xr.at[5 + part],
                {"dp": to},
            )
        own = block(doc, dp_rows)
        dp1r_s[part, own, :] = dp1_s[part, own, :]

    def reduce_second(part):
        take(dp1r_s.at[part, pl.ds(0, (nd - 1) * dp_rows), :], xr.at[5 + part])
        total = dp1r_s[part, pl.ds(0, dp_rows), :].astype(F32)
        for s in range(1, nd):
            total = total + dp1r_s[part, pl.ds(s * dp_rows, dp_rows), :].astype(F32)
        own = block(doc, dp_rows)
        dp2_s[part, own, :] = total
        for o in range(1, nd):
            send(
                dp2_s.at[part, own, :],
                dp2_s.at[part, own, :],
                xs.at[7 + part],
                xr.at[7 + part],
                {"dp": doc_peer(o)},
            )

    take(gv_s.at[pl.ds(0, most), :], xr.at[3])
    reduce_first(0, gv_s)
    take(gk_s.at[pl.ds(0, most), :], xr.at[4])
    reduce_first(1, gk_s)
    reduce_second(0)
    reduce_second(1)
    out_copies = []
    for part, out in ((0, vw_hbm), (1, kw_hbm)):
        take(dp2_s.at[part, pl.ds(0, (nd - 1) * dp_rows), :], xr.at[7 + part])
        copy = pltpu.make_async_copy(dp2_s.at[part], out, out_sem.at[3 + part])
        copy.start()
        out_copies.append(copy)

    take(kv_s.at[pl.ds(0, most), :], ag_send.at[0])
    take(fsl_s.at[pl.ds(0, most), :], xs.at[0])
    for index, ref in ((1, sendv_s), (2, sendk_s), (3, gv_s), (4, gk_s)):
        take(ref.at[pl.ds(0, most), :], xs.at[index])
    for part in range(2):
        take(dp1_s.at[part, pl.ds(0, (nd - 1) * dp_rows), :], xs.at[5 + part])
        take(dp2_s.at[part, pl.ds(0, (nd - 1) * dp_rows), :], xs.at[7 + part])
    for copy in [ctx_copy, qg_copy, fg_copy] + out_copies:
        copy.wait()


def local(ns, nd, queries, image_feats, key_weight, value_weight, image_pos, image_slot, ctx_grad):
    d, hd = key_weight.shape
    tokens, width = queries.shape[1:]
    vt = image_feats.shape[2]
    heads = width // hd
    keys = ns * vt
    chunk = GROUP_DEVICES * vt
    ds_cols = d // ns
    dp_rows = ds_cols // nd
    rows = heads * tokens

    def lanes(row, fill):
        return jnp.pad(row, ((0, 0), (0, hd - row.shape[1])), constant_values=fill)

    anywhere = pl.BlockSpec(memory_space=pl.ANY)
    inside = pl.BlockSpec(memory_space=pltpu.VMEM)
    outs = pl.pallas_call(
        functools.partial(kernel, ns, nd),
        out_shape=(
            jax.ShapeDtypeStruct((tokens, width), BF16),
            jax.ShapeDtypeStruct((tokens, width), BF16),
            jax.ShapeDtypeStruct((vt, d), BF16),
            jax.ShapeDtypeStruct((ds_cols, hd), F32),
            jax.ShapeDtypeStruct((ds_cols, hd), F32),
        ),
        in_specs=[anywhere] * 4 + [inside] * 2 + [anywhere],
        out_specs=[anywhere] * 5,
        scratch_shapes=[
            pltpu.VMEM((tokens, width), BF16),
            pltpu.VMEM((tokens, width), BF16),
            pltpu.VMEM((vt, d), BF16),
            pltpu.VMEM((d, 2 * hd), BF16),
            pltpu.VMEM((vt, hd), F32),
            pltpu.VMEM((keys, 2 * hd), BF16),
            pltpu.VMEM((rows, 2 * hd), BF16),
            pltpu.VMEM((rows, 2 * hd), BF16),
            pltpu.VMEM((hd, keys), BF16),
            pltpu.VMEM((hd, keys), BF16),
            pltpu.VMEM((keys, rows), BF16),
            pltpu.VMEM((heads, 2 * hd, tokens), F32),
            pltpu.VMEM((tokens, width), BF16),
            pltpu.VMEM((tokens, width), BF16),
            pltpu.VMEM((vt, d), BF16),
            pltpu.VMEM((keys, ds_cols), BF16),
            pltpu.VMEM((keys, hd), BF16),
            pltpu.VMEM((keys, hd), BF16),
            pltpu.VMEM((keys, hd), BF16),
            pltpu.VMEM((keys, hd), BF16),
            pltpu.VMEM((keys, hd), BF16),
            pltpu.VMEM((keys, hd), BF16),
            pltpu.VMEM((2, ds_cols, hd), BF16),
            pltpu.VMEM((2, ds_cols, hd), BF16),
            pltpu.VMEM((2, ds_cols, hd), F32),
            pltpu.SemaphoreType.DMA((14,)),
            pltpu.SemaphoreType.DMA((5,)),
            pltpu.SemaphoreType.DMA((1,)),
            pltpu.SemaphoreType.DMA((ns // GROUP_DEVICES,)),
            pltpu.SemaphoreType.DMA((9,)),
            pltpu.SemaphoreType.DMA((9,)),
        ],
        compiler_params=pltpu.CompilerParams(
            collective_id=0, has_side_effects=True, vmem_limit_bytes=56 * 1024 * 1024
        ),
    )(
        queries[0],
        image_feats.reshape(vt, d),
        key_weight,
        value_weight,
        lanes(image_pos, 0),
        lanes(image_slot, -1),
        ctx_grad[0],
    )
    context, query_grad, feats_grad, key_wgrad, value_wgrad = outs
    return (
        context[None],
        query_grad[None],
        feats_grad.reshape(1, 1, vt, d),
        key_wgrad,
        value_wgrad,
    )


def solution(mesh):
    return jax.shard_map(
        functools.partial(local, mesh.shape["seq"], mesh.shape["dp"]),
        mesh=mesh,
        in_specs=(
            P("dp", "seq", None),
            P("dp", "seq", None, None),
            P(),
            P(),
            P("dp", None),
            P("dp", None),
            P("dp", "seq", None),
        ),
        out_specs=(
            P("dp", "seq", None),
            P("dp", "seq", None),
            P("dp", "seq", None, None),
            P("seq", None),
            P("seq", None),
        ),
        check_vma=False,
    )
```

```python
import functools

import jax
import jax.numpy as jnp
from jax import lax
from jax.experimental import pallas as pl
from jax.experimental.pallas import tpu as pltpu
from jax.sharding import PartitionSpec as P

NORM_EPS = 1e-05
LOG2E = 1.4426950408889634
HIDE = -30000.0
GROUP_DEVICES = 4
SPAN = 8
EARLY, LATER, CUT = 28, 28, 5
KV, FEATS, VSUM, KSUM, VALL, KALL, SUM1, SUM2, BOTH = 0, 1, 2, 3, 4, 5, 6, 8, 10
BF16 = jnp.bfloat16
F32 = jnp.float32
MESH = pl.DeviceIdType.MESH
ACROSS = (((1,), (1,)), ((), ()))


def dot(a, b):
    return jnp.dot(a, b, preferred_element_type=F32)


def dot_across(a, b):
    return lax.dot_general(a, b, ACROSS, preferred_element_type=F32)


def row_factor(rows):
    return lax.rsqrt(jnp.mean(rows * rows, axis=-1, keepdims=True) + NORM_EPS)


def norm_back(rows, upstream):
    factor = row_factor(rows)
    normed = rows * factor
    return factor * (upstream - normed * jnp.mean(upstream * normed, axis=-1, keepdims=True))


def kernel(
    ns,
    nd,
    q_hbm,
    f_hbm,
    wk_hbm,
    wv_hbm,
    pos_ref,
    slot_ref,
    c_hbm,
    ctx_hbm,
    qg_hbm,
    fg_hbm,
    kw_hbm,
    vw_hbm,
    q_s,
    c_s,
    f_s,
    w_s,
    key_s,
    kv_s,
    y_s,
    do_s,
    vt_s,
    kt_s,
    e_s,
    ot_s,
    ctx_s,
    qg_s,
    fg_s,
    fsl_s,
    sendv_s,
    sendk_s,
    rsv_s,
    rsk_s,
    gv_s,
    gk_s,
    dp1_s,
    dp1r_s,
    dp2_s,
    wg_s,
    in_sem,
    out_sem,
    ag_recv,
    xs,
    xr,
):
    tokens, width = q_s.shape
    hd = 128
    heads = width // hd
    vt, d = f_s.shape
    ds_cols = d // ns
    chunk = GROUP_DEVICES * vt
    ng = ns // GROUP_DEVICES
    keys = ns * vt
    scale = hd ** (-0.5)
    half = ds_cols // 2
    nx = ns // SPAN
    nz = nd // 2

    me = lax.axis_index("seq")
    doc = lax.axis_index("dp")
    my_group = lax.div(me, GROUP_DEVICES)
    my_place = lax.rem(me, GROUP_DEVICES)
    my_x = lax.div(me, SPAN)
    my_r = lax.rem(me, SPAN)
    my_zone = lax.div(doc, 2)
    my_core = lax.rem(doc, 2)

    def peer(g, j):
        return lax.rem(my_group + g, ng) * GROUP_DEVICES + lax.rem(my_place + j, GROUP_DEVICES)

    def span_peer(j):
        return lax.rem(my_r + j, SPAN)

    def zone_peer(o):
        return {"dp": lax.rem(my_zone + o, nz) * 2 + my_core}

    other_core = {"dp": my_zone * 2 + 1 - my_core}

    def block(index, size):
        return pl.ds(pl.multiple_of(index * size, size), size)

    pairs = [(g, j) for g in range(ng) for j in range(GROUP_DEVICES) if (g, j) != (0, 0)]

    steps = 4
    depth = d // steps
    w_copies = []
    for k in range(steps):
        rows = pl.ds(k * depth, depth)
        w_copies.append(
            (
                pltpu.make_async_copy(f_hbm.at[:, rows], f_s.at[:, rows], in_sem.at[3 * k]),
                pltpu.make_async_copy(
                    wk_hbm.at[rows, :], w_s.at[rows, pl.ds(0, hd)], in_sem.at[3 * k + 1]
                ),
                pltpu.make_async_copy(
                    wv_hbm.at[rows, :], w_s.at[rows, pl.ds(hd, hd)], in_sem.at[3 * k + 2]
                ),
            )
        )
    q_copy = pltpu.make_async_copy(q_hbm, q_s, in_sem.at[3 * steps])
    c_copy = pltpu.make_async_copy(c_hbm, c_s, in_sem.at[3 * steps + 1])
    for copies in w_copies:
        for copy in copies:
            copy.start()
    q_copy.start()
    c_copy.start()

    barrier = pltpu.get_barrier_semaphore()
    lines = [(i, k) for i in range(nx) for k in range(2) if (i, k) != (0, 0)]
    columns = [(j, x) for j in range(1, SPAN) for x in range(nx)]

    def line_peer(i, k):
        return lax.rem(my_x + i, nx), lax.rem(my_core + k, 2)

    def line_device(i, k):
        x, core = line_peer(i, k)
        return {"dp": my_zone * 2 + core, "seq": x * SPAN + my_r}

    def greet(device):
        pl.semaphore_signal(barrier, inc=1, device_id=device, device_id_type=MESH)

    for o in range(1, nz):
        greet(zone_peer(o))
    for i, k in lines:
        if k:
            greet(line_device(i, k))
    for g, j in reversed(pairs):
        greet({"seq": peer(g, j)})
    greeted = ns - 1 + nx + nz - 1

    mine = block(me, vt)

    def send(phase, src, dst, target, arrival=None):
        pltpu.make_async_remote_copy(
            src_ref=src,
            dst_ref=dst,
            send_sem=xs.at[phase],
            recv_sem=xr.at[phase] if arrival is None else arrival,
            device_id=target,
            device_id_type=MESH,
        ).start()

    def take(phase, ref, arrival=None):
        pltpu.make_async_copy(ref, ref, xr.at[phase] if arrival is None else arrival).wait()

    def sent(phase, ref):
        pltpu.make_async_copy(ref, ref, xs.at[phase]).wait()

    def send_feats(some):
        for j, x in some:
            to = span_peer(j)
            send(
                FEATS,
                f_hbm.at[:, block(x * SPAN + to, ds_cols)],
                fsl_s.at[block(my_r, vt), pl.ds(x * ds_cols, ds_cols)],
                {"seq": my_x * SPAN + to},
            )

    rows_kv = jnp.zeros((vt, 2 * hd), F32)
    for k in range(steps):
        for copy in w_copies[k]:
            copy.wait()
        rows = pl.ds(k * depth, depth)
        rows_kv = rows_kv + dot(f_s[:, rows], w_s[rows, :])
    key_rows = rows_kv[:, :hd]
    key_s[...] = key_rows
    kv_s[mine, :] = jnp.concatenate(
        [(key_rows * row_factor(key_rows)).astype(BF16), rows_kv[:, hd:].astype(BF16)], axis=1
    )
    lane = lax.broadcasted_iota(jnp.int32, (tokens, hd), 1)
    tok = me * tokens + lax.broadcasted_iota(jnp.int32, (tokens, hd), 0)
    rest = hd - pos_ref.shape[1]
    positions = jnp.concatenate([pos_ref[...], jnp.zeros((1, rest), jnp.int32)], axis=1)
    slots = jnp.concatenate([slot_ref[...], jnp.full((1, rest), -1, jnp.int32)], axis=1)
    hidden = jnp.where(positions > tok, HIDE, 0.0).astype(BF16)
    q_copy.wait()
    for h in range(heads):
        raw = q_s[:, pl.ds(h * hd, hd)].astype(F32)
        rows = pl.ds(h * tokens, tokens)
        y_s[rows, pl.ds(0, hd)] = (raw * row_factor(raw)).astype(BF16)
        y_s[rows, pl.ds(hd, hd)] = hidden

    pl.semaphore_wait(barrier, greeted)
    for g, j in pairs:
        send(KV, kv_s.at[mine, :], kv_s.at[mine, :], {"seq": peer(g, j)}, ag_recv.at[g])
    send_feats(columns[:EARLY])
    for x in range(nx):
        cols = block(x * SPAN + my_r, ds_cols)
        fsl_s[block(my_r, vt), pl.ds(x * ds_cols, ds_cols)] = f_s[:, cols]

    def first_pass(g, first):
        group = lax.rem(my_group - g + ng, ng)
        rows = block(group, chunk)
        pair = kv_s[rows, :]
        slot_of_key = group * GROUP_DEVICES + lax.div(
            lax.broadcasted_iota(jnp.int32, (chunk, hd), 0), vt
        )
        marks = (slots == slot_of_key).astype(F32).astype(BF16)
        key_aug = jnp.concatenate([pair[:, :hd], marks], axis=1)
        value_t = pair[:, hd:].astype(F32).T.astype(BF16)
        kt_s[:, rows] = pair[:, :hd].astype(F32).T.astype(BF16)
        value_aug = jnp.concatenate([value_t, jnp.ones((hd, chunk), BF16)], axis=0)
        for h in range(heads):
            head = pl.ds(h * tokens, tokens)
            scores = dot_across(key_aug, y_s[head, :])
            weights = jnp.exp2(scores * (scale * LOG2E)).astype(BF16)
            e_s[rows, head] = weights
            part = dot(value_aug, weights)
            if first:
                ot_s[h] = part
            else:
                ot_s[h] += part

    take(KV, kv_s.at[pl.ds(0, chunk - vt), :], ag_recv.at[0])
    first_pass(0, True)

    def first_step(g, carry):
        take(KV, kv_s.at[pl.ds(0, chunk), :], ag_recv.at[g])
        first_pass(g, False)
        return carry

    lax.fori_loop(1, ng, first_step, 0)

    send_feats(columns[EARLY:LATER])

    c_copy.wait()
    for h in range(heads):
        cols = pl.ds(h * hd, hd)
        both = ot_s[h].T
        inverse = 1.0 / both[:, hd:]
        context = both[:, :hd] * inverse
        ctx_s[:, cols] = context.astype(BF16)
        scaled = (c_s[:, cols].astype(F32) * inverse).astype(BF16)
        centre = -jnp.sum(context * scaled.astype(F32), axis=1, keepdims=True)
        high = centre.astype(BF16).astype(F32)
        low = centre - high
        extra = jnp.where(lane == 0, high, jnp.where(lane == 1, low, 0.0)).astype(BF16)
        rows = pl.ds(h * tokens, tokens)
        do_s[rows, pl.ds(0, hd)] = scaled
        do_s[rows, pl.ds(hd, hd)] = extra
    ctx_copy = pltpu.make_async_copy(ctx_s, ctx_hbm, out_sem.at[0])
    ctx_copy.start()

    def send_group(phase, src, dst, group, first):
        for j in range(first, GROUP_DEVICES):
            to = group * GROUP_DEVICES + lax.rem(my_place + j, GROUP_DEVICES)
            send(phase, src.at[block(to, vt), :], dst.at[mine, :], {"seq": to})

    def value_part(group):
        rows = block(group, chunk)
        sendv_s[rows, :] = dot(e_s[rows, :], do_s[:, pl.ds(0, hd)]).astype(BF16)

    def value_step(g, carry):
        group = lax.rem(my_group + g, ng)
        value_part(group)
        send_group(VSUM, sendv_s, rsv_s, group, 0)
        return carry

    lax.fori_loop(1, ng, value_step, 0)
    value_part(my_group)
    send_group(VSUM, sendv_s, rsv_s, my_group, 1)
    rsv_s[mine, :] = sendv_s[mine, :]

    lane_of_key = lax.broadcasted_iota(jnp.int32, (chunk, hd), 1)
    ones_two = jnp.where(lane_of_key < 2, 1.0, 0.0).astype(BF16)

    def key_part(group):
        rows = block(group, chunk)
        value_aug = jnp.concatenate([kv_s[rows, pl.ds(hd, hd)], ones_two], axis=1)
        for h in range(heads):
            head = pl.ds(h * tokens, tokens)
            part = dot_across(value_aug, do_s[head, :])
            e_s[rows, head] = (e_s[rows, head].astype(F32) * part).astype(BF16)
        sendk_s[rows, :] = (dot(e_s[rows, :], y_s[:, pl.ds(0, hd)]) * scale).astype(BF16)

    def key_step(g, carry):
        group = lax.rem(my_group + g, ng)
        key_part(group)
        send_group(KSUM, sendk_s, rsk_s, group, 0)
        return carry

    def add_up(ref, size):
        total = ref[pl.ds(0, size), :].astype(F32)
        for s in range(1, ref.shape[0] // size):
            total = total + ref[pl.ds(s * size, size), :].astype(F32)
        return total

    most = (ns - 1) * vt
    span_most = (SPAN - 1) * vt
    own = block(my_r, vt)

    def send_all(phase, ref):
        for j in range(1, SPAN):
            send(phase, ref.at[own, :], ref.at[own, :], {"seq": my_x * SPAN + span_peer(j)})

    lax.fori_loop(1, CUT, key_step, 0)

    take(VSUM, rsv_s.at[pl.ds(0, most), :])
    gv_s[own, :] = add_up(rsv_s, vt).astype(BF16)
    send_all(VALL, gv_s)

    lax.fori_loop(CUT, ng, key_step, 0)
    key_part(my_group)
    send_group(KSUM, sendk_s, rsk_s, my_group, 1)
    rsk_s[mine, :] = sendk_s[mine, :]
    send_feats(columns[LATER:])

    for h in range(heads):
        cols = pl.ds(h * hd, hd)
        upstream = dot(kt_s[...], e_s[:, pl.ds(h * tokens, tokens)]).T * scale
        qg_s[:, cols] = norm_back(q_s[:, cols].astype(F32), upstream).astype(BF16)
    qg_copy = pltpu.make_async_copy(qg_s, qg_hbm, out_sem.at[1])
    qg_copy.start()

    def sum_first(part, grads):
        dp1_s[part] = dot(feats_t, grads[...]).astype(BF16)
        for i, k in lines:
            x, core = line_peer(i, k)
            send(
                SUM1 + part,
                dp1_s.at[part, block(x * 2 + core, half), :],
                dp1r_s.at[part, block(my_x * 2 + my_core, half), :],
                line_device(i, k),
            )
        slot = block(my_x * 2 + my_core, half)
        dp1r_s[part, slot, :] = dp1_s[part, slot, :]

    def sum_second(part):
        take(SUM1 + part, dp1r_s.at[part, pl.ds(0, len(lines) * half), :])
        slot = block(my_zone, half)
        dp2_s[part, slot, :] = add_up(dp1r_s.at[part], half).astype(BF16)
        for o in range(1, nz):
            send(SUM2 + part, dp2_s.at[part, slot, :], dp2_s.at[part, slot, :], zone_peer(o))

    def sum_third(part):
        if nz > 1:
            take(SUM2 + part, dp2_s.at[part, pl.ds(0, (nz - 1) * half), :])
        slot = block(my_core, half)
        wg_s[part, slot, :] = add_up(dp2_s.at[part], half)
        send(BOTH + part, wg_s.at[part, slot, :], wg_s.at[part, slot, :], other_core)

    def sum_last(part, out):
        take(BOTH + part, wg_s.at[part, pl.ds(0, half), :])
        copy = pltpu.make_async_copy(wg_s.at[part], out, out_sem.at[3 + part])
        copy.start()
        return copy

    take(FEATS, fsl_s.at[pl.ds(0, span_most), :])
    feats_t = fsl_s[...].astype(F32).T.astype(BF16)
    take(VALL, gv_s.at[pl.ds(0, span_most), :])
    sum_first(0, gv_s)

    take(KSUM, rsk_s.at[pl.ds(0, most), :])
    gk_s[own, :] = norm_back(key_s[...], add_up(rsk_s, vt)).astype(BF16)
    send_all(KALL, gk_s)

    row_grads = jnp.concatenate([gk_s[own, :], gv_s[own, :]], axis=1)
    for k in range(steps):
        rows = pl.ds(k * depth, depth)
        fg_s[:, rows] = dot_across(row_grads, w_s[rows, :]).astype(BF16)
    fg_copy = pltpu.make_async_copy(fg_s, fg_hbm, out_sem.at[2])
    fg_copy.start()

    sum_second(0)
    take(KALL, gk_s.at[pl.ds(0, span_most), :])
    sum_first(1, gk_s)
    sum_third(0)
    sum_second(1)
    out_copies = [sum_last(0, vw_hbm)]
    sum_third(1)
    out_copies.append(sum_last(1, kw_hbm))

    for phase, ref in ((KV, kv_s), (VSUM, sendv_s), (KSUM, sendk_s)):
        sent(phase, ref.at[pl.ds(0, most), :])
    for phase, ref in ((FEATS, fsl_s), (VALL, gv_s), (KALL, gk_s)):
        sent(phase, ref.at[pl.ds(0, span_most), :])
    for part in range(2):
        sent(SUM1 + part, dp1_s.at[part, pl.ds(0, len(lines) * half), :])
        if nz > 1:
            sent(SUM2 + part, dp2_s.at[part, pl.ds(0, (nz - 1) * half), :])
        sent(BOTH + part, wg_s.at[part, pl.ds(0, half), :])
    for copy in [ctx_copy, qg_copy, fg_copy] + out_copies:
        copy.wait()


def hand_over(*refs):
    count = len(refs) // 3
    sems = refs[-1]
    arrivals, departures = [], []
    for i in range(count):
        held = refs[2 * count + i]
        arrivals.append(pltpu.make_async_copy(refs[i], held, sems.at[0, i]))
        departures.append(pltpu.make_async_copy(held, refs[count + i], sems.at[1, i]))
    for copy in arrivals:
        copy.start()
    for arrival, departure in zip(arrivals, departures):
        arrival.wait()
        departure.start()
    for copy in departures:
        copy.wait()


def local(ns, nd, queries, image_feats, key_weight, value_weight, image_pos, image_slot, ctx_grad):
    d, hd = key_weight.shape
    tokens, width = queries.shape[1:]
    vt = image_feats.shape[2]
    heads = width // hd
    keys = ns * vt
    chunk = GROUP_DEVICES * vt
    ds_cols = d // ns
    nx = ns // SPAN
    rows = heads * tokens

    anywhere = pl.BlockSpec(memory_space=pl.ANY)
    inside = pl.BlockSpec(memory_space=pltpu.VMEM)
    outs = pl.pallas_call(
        functools.partial(kernel, ns, nd),
        out_shape=(
            jax.ShapeDtypeStruct((tokens, width), BF16),
            jax.ShapeDtypeStruct((tokens, width), BF16),
            jax.ShapeDtypeStruct((vt, d), BF16),
            jax.ShapeDtypeStruct((ds_cols, hd), F32),
            jax.ShapeDtypeStruct((ds_cols, hd), F32),
        ),
        in_specs=[anywhere] * 4 + [inside] * 2 + [anywhere],
        out_specs=[anywhere] * 5,
        scratch_shapes=[
            pltpu.VMEM((tokens, width), BF16),
            pltpu.VMEM((tokens, width), BF16),
            pltpu.VMEM((vt, d), BF16),
            pltpu.VMEM((d, 2 * hd), BF16),
            pltpu.VMEM((vt, hd), F32),
            pltpu.VMEM((keys, 2 * hd), BF16),
            pltpu.VMEM((rows, 2 * hd), BF16),
            pltpu.VMEM((rows, 2 * hd), BF16),
            pltpu.VMEM((hd, keys), BF16),
            pltpu.VMEM((hd, keys), BF16),
            pltpu.VMEM((keys, rows), BF16),
            pltpu.VMEM((heads, 2 * hd, tokens), F32),
            pltpu.VMEM((tokens, width), BF16),
            pltpu.VMEM((tokens, width), BF16),
            pltpu.VMEM((vt, d), BF16),
            pltpu.VMEM((SPAN * vt, nx * ds_cols), BF16),
            pltpu.VMEM((keys, hd), BF16),
            pltpu.VMEM((keys, hd), BF16),
            pltpu.VMEM((keys, hd), BF16),
            pltpu.VMEM((keys, hd), BF16),
            pltpu.VMEM((SPAN * vt, hd), BF16),
            pltpu.VMEM((SPAN * vt, hd), BF16),
            pltpu.VMEM((2, nx * ds_cols, hd), BF16),
            pltpu.VMEM((2, nx * ds_cols, hd), BF16),
            pltpu.VMEM((2, nd // 2 * ds_cols // 2, hd), BF16),
            pltpu.VMEM((2, ds_cols, hd), F32),
            pltpu.SemaphoreType.DMA((14,)),
            pltpu.SemaphoreType.DMA((5,)),
            pltpu.SemaphoreType.DMA((ns // GROUP_DEVICES,)),
            pltpu.SemaphoreType.DMA((12,)),
            pltpu.SemaphoreType.DMA((12,)),
        ],
        compiler_params=pltpu.CompilerParams(
            collective_id=0, has_side_effects=True, vmem_limit_bytes=56 * 1024 * 1024
        ),
    )(
        queries[0],
        image_feats.reshape(vt, d),
        key_weight,
        value_weight,
        image_pos,
        image_slot,
        ctx_grad[0],
    )
    context, query_grad, feats_grad, key_wgrad, value_wgrad = pl.pallas_call(
        hand_over,
        out_shape=tuple(jax.ShapeDtypeStruct(out.shape, out.dtype) for out in outs),
        in_specs=[anywhere] * 5,
        out_specs=[anywhere] * 5,
        scratch_shapes=[pltpu.VMEM(out.shape, out.dtype) for out in outs]
        + [pltpu.SemaphoreType.DMA((2, 5))],
        compiler_params=pltpu.CompilerParams(vmem_limit_bytes=60 * 1024 * 1024),
    )(*outs)
    return (
        context[None],
        query_grad[None],
        feats_grad.reshape(1, 1, vt, d),
        key_wgrad,
        value_wgrad,
    )


def solution(mesh):
    return jax.shard_map(
        functools.partial(local, mesh.shape["seq"], mesh.shape["dp"]),
        mesh=mesh,
        in_specs=(
            P("dp", "seq", None),
            P("dp", "seq", None, None),
            P(),
            P(),
            P("dp", None),
            P("dp", None),
            P("dp", "seq", None),
        ),
        out_specs=(
            P("dp", "seq", None),
            P("dp", "seq", None),
            P("dp", "seq", None, None),
            P("seq", None),
            P("seq", None),
        ),
        check_vma=False,
    )
```

```python
import functools

import jax
import jax.numpy as jnp
from jax import lax
from jax.experimental import pallas as pl
from jax.experimental.pallas import tpu as pltpu
from jax.sharding import PartitionSpec as P

NORM_EPS = 1e-05
LOG2E = 1.4426950408889634
HIDE = -30000.0
GROUP_DEVICES = 4
SPAN = 8
PIECES = 1
KV, FEATS, VSUM, KSUM, VALL, KALL, SUM1, SUM2, BOTH = 0, 1, 2, 3, 4, 5, 6, 8, 10
BF16 = jnp.bfloat16
F32 = jnp.float32
MESH = pl.DeviceIdType.MESH
ACROSS = (((1,), (1,)), ((), ()))


def dot(a, b):
    return jnp.dot(a, b, preferred_element_type=F32)


def dot_across(a, b):
    return lax.dot_general(a, b, ACROSS, preferred_element_type=F32)


def row_factor(rows):
    return lax.rsqrt(jnp.mean(rows * rows, axis=-1, keepdims=True) + NORM_EPS)


def norm_back(rows, upstream):
    factor = row_factor(rows)
    normed = rows * factor
    return factor * (upstream - normed * jnp.mean(upstream * normed, axis=-1, keepdims=True))


def kernel(
    ns,
    nd,
    q_hbm,
    f_hbm,
    wk_hbm,
    wv_hbm,
    pos_ref,
    slot_ref,
    c_hbm,
    ctx_hbm,
    qg_hbm,
    fg_hbm,
    kw_hbm,
    vw_hbm,
    q_s,
    c_s,
    f_s,
    w_s,
    key_s,
    kv_s,
    y_s,
    do_s,
    vt_s,
    kt_s,
    e_s,
    ot_s,
    ctx_s,
    qg_s,
    fg_s,
    fsl_s,
    sendv_s,
    sendk_s,
    rsv_s,
    rsk_s,
    gv_s,
    gk_s,
    dp1_s,
    dp1r_s,
    dp2_s,
    wg_s,
    in_sem,
    out_sem,
    ag_recv,
    xs,
    xr,
):
    tokens, width = q_s.shape
    hd = 128
    heads = width // hd
    vt, d = f_s.shape
    ds_cols = d // ns
    chunk = GROUP_DEVICES * vt
    ng = ns // GROUP_DEVICES
    keys = ns * vt
    scale = hd ** (-0.5)
    half = ds_cols // 2
    nx = ns // SPAN
    nz = nd // 2

    me = lax.axis_index("seq")
    doc = lax.axis_index("dp")
    my_group = lax.div(me, GROUP_DEVICES)
    my_place = lax.rem(me, GROUP_DEVICES)
    my_x = lax.div(me, SPAN)
    my_r = lax.rem(me, SPAN)
    my_zone = lax.div(doc, 2)
    my_core = lax.rem(doc, 2)

    def peer(g, j):
        return lax.rem(my_group + g, ng) * GROUP_DEVICES + lax.rem(my_place + j, GROUP_DEVICES)

    def span_peer(j):
        return lax.rem(my_r + j, SPAN)

    def zone_peer(o):
        return {"dp": lax.rem(my_zone + o, nz) * 2 + my_core}

    other_core = {"dp": my_zone * 2 + 1 - my_core}

    def block(index, size):
        return pl.ds(pl.multiple_of(index * size, size), size)

    pairs = [(g, j) for g in range(ng) for j in range(GROUP_DEVICES) if (g, j) != (0, 0)]

    steps = 4
    depth = d // steps
    w_copies = []
    for k in range(steps):
        rows = pl.ds(k * depth, depth)
        w_copies.append(
            (
                pltpu.make_async_copy(f_hbm.at[:, rows], f_s.at[:, rows], in_sem.at[3 * k]),
                pltpu.make_async_copy(
                    wk_hbm.at[rows, :], w_s.at[rows, pl.ds(0, hd)], in_sem.at[3 * k + 1]
                ),
                pltpu.make_async_copy(
                    wv_hbm.at[rows, :], w_s.at[rows, pl.ds(hd, hd)], in_sem.at[3 * k + 2]
                ),
            )
        )
    q_copy = pltpu.make_async_copy(q_hbm, q_s, in_sem.at[3 * steps])
    c_copy = pltpu.make_async_copy(c_hbm, c_s, in_sem.at[3 * steps + 1])
    for copies in w_copies:
        for copy in copies:
            copy.start()
    q_copy.start()
    c_copy.start()

    barrier = pltpu.get_barrier_semaphore()
    lines = [(i, k) for i in range(nx) for k in range(2) if (i, k) != (0, 0)]
    columns = [(j, x) for j in range(1, SPAN) for x in range(nx)]

    def line_peer(i, k):
        return lax.rem(my_x + i, nx), lax.rem(my_core + k, 2)

    def line_device(i, k):
        x, core = line_peer(i, k)
        return {"dp": my_zone * 2 + core, "seq": x * SPAN + my_r}

    def greet(device):
        pl.semaphore_signal(barrier, inc=1, device_id=device, device_id_type=MESH)

    for o in range(1, nz):
        greet(zone_peer(o))
    for i, k in lines:
        if k:
            greet(line_device(i, k))
    for g, j in reversed(pairs):
        greet({"seq": peer(g, j)})
    greeted = ns - 1 + nx + nz - 1

    mine = block(me, vt)

    def send(phase, src, dst, target, arrival=None):
        pltpu.make_async_remote_copy(
            src_ref=src,
            dst_ref=dst,
            send_sem=xs.at[phase],
            recv_sem=xr.at[phase] if arrival is None else arrival,
            device_id=target,
            device_id_type=MESH,
        ).start()

    def take(phase, ref, arrival=None):
        pltpu.make_async_copy(ref, ref, xr.at[phase] if arrival is None else arrival).wait()

    def sent(phase, ref):
        pltpu.make_async_copy(ref, ref, xs.at[phase]).wait()

    def send_feats(some):
        for j, x in some:
            to = span_peer(j)
            send(
                FEATS,
                f_hbm.at[:, block(x * SPAN + to, ds_cols)],
                fsl_s.at[block(my_r, vt), pl.ds(x * ds_cols, ds_cols)],
                {"seq": my_x * SPAN + to},
            )

    rows_kv = jnp.zeros((vt, 2 * hd), F32)
    for k in range(steps):
        for copy in w_copies[k]:
            copy.wait()
        rows = pl.ds(k * depth, depth)
        rows_kv = rows_kv + dot(f_s[:, rows], w_s[rows, :])
    key_rows = rows_kv[:, :hd]
    key_s[...] = key_rows
    kv_s[mine, :] = jnp.concatenate(
        [(key_rows * row_factor(key_rows)).astype(BF16), rows_kv[:, hd:].astype(BF16)], axis=1
    )
    lane = lax.broadcasted_iota(jnp.int32, (tokens, hd), 1)
    tok = me * tokens + lax.broadcasted_iota(jnp.int32, (tokens, hd), 0)
    rest = hd - pos_ref.shape[1]
    positions = jnp.concatenate([pos_ref[...], jnp.zeros((1, rest), jnp.int32)], axis=1)
    slots = jnp.concatenate([slot_ref[...], jnp.full((1, rest), -1, jnp.int32)], axis=1)
    hidden = jnp.where(positions > tok, HIDE, 0.0).astype(BF16)
    q_copy.wait()
    for h in range(heads):
        raw = q_s[:, pl.ds(h * hd, hd)].astype(F32)
        rows = pl.ds(h * tokens, tokens)
        y_s[rows, pl.ds(0, hd)] = (raw * row_factor(raw)).astype(BF16)
        y_s[rows, pl.ds(hd, hd)] = hidden

    pl.semaphore_wait(barrier, greeted)
    for g, j in pairs:
        send(KV, kv_s.at[mine, :], kv_s.at[mine, :], {"seq": peer(g, j)}, ag_recv.at[g])
    send_feats(columns)
    for x in range(nx):
        cols = block(x * SPAN + my_r, ds_cols)
        fsl_s[block(my_r, vt), pl.ds(x * ds_cols, ds_cols)] = f_s[:, cols]

    def first_pass(g, first):
        group = lax.rem(my_group - g + ng, ng)
        rows = block(group, chunk)
        pair = kv_s[rows, :]
        slot_of_key = group * GROUP_DEVICES + lax.div(
            lax.broadcasted_iota(jnp.int32, (chunk, hd), 0), vt
        )
        marks = (slots == slot_of_key).astype(F32).astype(BF16)
        key_aug = jnp.concatenate([pair[:, :hd], marks], axis=1)
        value_t = pair[:, hd:].astype(F32).T.astype(BF16)
        kt_s[:, rows] = pair[:, :hd].astype(F32).T.astype(BF16)
        value_aug = jnp.concatenate([value_t, jnp.ones((hd, chunk), BF16)], axis=0)
        for h in range(heads):
            head = pl.ds(h * tokens, tokens)
            scores = dot_across(key_aug, y_s[head, :])
            weights = jnp.exp2(scores * (scale * LOG2E)).astype(BF16)
            e_s[rows, head] = weights
            part = dot(value_aug, weights)
            if first:
                ot_s[h] = part
            else:
                ot_s[h] += part

    take(KV, kv_s.at[pl.ds(0, chunk - vt), :], ag_recv.at[0])
    first_pass(0, True)

    def first_step(g, carry):
        take(KV, kv_s.at[pl.ds(0, chunk), :], ag_recv.at[g])
        first_pass(g, False)
        return carry

    lax.fori_loop(1, ng, first_step, 0)


    c_copy.wait()
    for h in range(heads):
        cols = pl.ds(h * hd, hd)
        both = ot_s[h].T
        inverse = 1.0 / both[:, hd:]
        context = both[:, :hd] * inverse
        ctx_s[:, cols] = context.astype(BF16)
        scaled = (c_s[:, cols].astype(F32) * inverse).astype(BF16)
        centre = -jnp.sum(context * scaled.astype(F32), axis=1, keepdims=True)
        high = centre.astype(BF16).astype(F32)
        low = centre - high
        extra = jnp.where(lane == 0, high, jnp.where(lane == 1, low, 0.0)).astype(BF16)
        rows = pl.ds(h * tokens, tokens)
        do_s[rows, pl.ds(0, hd)] = scaled
        do_s[rows, pl.ds(hd, hd)] = extra
    ctx_copy = pltpu.make_async_copy(ctx_s, ctx_hbm, out_sem.at[0])
    ctx_copy.start()

    def send_group(phase, src, dst, group, first):
        for j in range(first, GROUP_DEVICES):
            to = group * GROUP_DEVICES + lax.rem(my_place + j, GROUP_DEVICES)
            send(phase, src.at[block(to, vt), :], dst.at[mine, :], {"seq": to})

    def value_part(group):
        rows = block(group, chunk)
        sendv_s[rows, :] = dot(e_s[rows, :], do_s[:, pl.ds(0, hd)]).astype(BF16)

    def value_step(g, carry):
        group = lax.rem(my_group + g, ng)
        value_part(group)
        send_group(VSUM, sendv_s, rsv_s, group, 0)
        return carry

    lax.fori_loop(1, ng, value_step, 0)
    value_part(my_group)
    send_group(VSUM, sendv_s, rsv_s, my_group, 1)
    rsv_s[mine, :] = sendv_s[mine, :]

    lane_of_key = lax.broadcasted_iota(jnp.int32, (chunk, hd), 1)
    ones_two = jnp.where(lane_of_key < 2, 1.0, 0.0).astype(BF16)

    def key_part(group):
        rows = block(group, chunk)
        value_aug = jnp.concatenate([kv_s[rows, pl.ds(hd, hd)], ones_two], axis=1)
        for h in range(heads):
            head = pl.ds(h * tokens, tokens)
            part = dot_across(value_aug, do_s[head, :])
            e_s[rows, head] = (e_s[rows, head].astype(F32) * part).astype(BF16)
        sendk_s[rows, :] = (dot(e_s[rows, :], y_s[:, pl.ds(0, hd)]) * scale).astype(BF16)

    def key_step(g, carry):
        group = lax.rem(my_group + g, ng)
        key_part(group)
        send_group(KSUM, sendk_s, rsk_s, group, 0)
        return carry

    def add_up(ref, size):
        total = ref[pl.ds(0, size), :].astype(F32)
        for s in range(1, ref.shape[0] // size):
            total = total + ref[pl.ds(s * size, size), :].astype(F32)
        return total

    most = (ns - 1) * vt
    span_most = (SPAN - 1) * vt
    own = block(my_r, vt)

    def send_all(phase, ref):
        for j in range(1, SPAN):
            send(phase, ref.at[own, :], ref.at[own, :], {"seq": my_x * SPAN + span_peer(j)})

    lax.fori_loop(1, ng, key_step, 0)
    key_part(my_group)
    send_group(KSUM, sendk_s, rsk_s, my_group, 1)
    rsk_s[mine, :] = sendk_s[mine, :]

    take(VSUM, rsv_s.at[pl.ds(0, most), :])
    gv_s[own, :] = add_up(rsv_s, vt).astype(BF16)
    send_all(VALL, gv_s)

    for h in range(heads):
        cols = pl.ds(h * hd, hd)
        upstream = dot(kt_s[...], e_s[:, pl.ds(h * tokens, tokens)]).T * scale
        qg_s[:, cols] = norm_back(q_s[:, cols].astype(F32), upstream).astype(BF16)
    qg_copy = pltpu.make_async_copy(qg_s, qg_hbm, out_sem.at[1])
    qg_copy.start()

    def sum_first(part, grads):
        dp1_s[part] = dot(feats_t, grads[...]).astype(BF16)
        for i, k in lines:
            x, core = line_peer(i, k)
            send(
                SUM1 + part,
                dp1_s.at[part, block(x * 2 + core, half), :],
                dp1r_s.at[part, block(my_x * 2 + my_core, half), :],
                line_device(i, k),
            )
        slot = block(my_x * 2 + my_core, half)
        dp1r_s[part, slot, :] = dp1_s[part, slot, :]

    def sum_second(part):
        take(SUM1 + part, dp1r_s.at[part, pl.ds(0, len(lines) * half), :])
        slot = block(my_zone, half)
        dp2_s[part, slot, :] = add_up(dp1r_s.at[part], half).astype(BF16)
        for o in range(1, nz):
            send(SUM2 + part, dp2_s.at[part, slot, :], dp2_s.at[part, slot, :], zone_peer(o))

    def sum_third(part):
        if nz > 1:
            take(SUM2 + part, dp2_s.at[part, pl.ds(0, (nz - 1) * half), :])
        slot = block(my_core, half)
        wg_s[part, slot, :] = add_up(dp2_s.at[part], half)
        send(BOTH + part, wg_s.at[part, slot, :], wg_s.at[part, slot, :], other_core)

    def sum_last(part, out):
        take(BOTH + part, wg_s.at[part, pl.ds(0, half), :])
        copy = pltpu.make_async_copy(wg_s.at[part], out, out_sem.at[3 + part])
        copy.start()
        return copy

    take(KSUM, rsk_s.at[pl.ds(0, most), :])
    gk_s[own, :] = norm_back(key_s[...], add_up(rsk_s, vt)).astype(BF16)
    send_all(KALL, gk_s)

    take(FEATS, fsl_s.at[pl.ds(0, span_most), :])
    feats_t = fsl_s[...].astype(F32).T.astype(BF16)
    take(VALL, gv_s.at[pl.ds(0, span_most), :])
    sum_first(0, gv_s)

    row_grads = jnp.concatenate([gk_s[own, :], gv_s[own, :]], axis=1)
    for k in range(steps):
        rows = pl.ds(k * depth, depth)
        fg_s[:, rows] = dot_across(row_grads, w_s[rows, :]).astype(BF16)
    fg_copy = pltpu.make_async_copy(fg_s, fg_hbm, out_sem.at[2])
    fg_copy.start()

    take(KALL, gk_s.at[pl.ds(0, span_most), :])
    sum_first(1, gk_s)
    sum_second(0)
    sum_second(1)
    sum_third(0)
    sum_third(1)
    out_copies = [sum_last(0, vw_hbm), sum_last(1, kw_hbm)]

    for phase, ref in ((KV, kv_s), (VSUM, sendv_s), (KSUM, sendk_s)):
        sent(phase, ref.at[pl.ds(0, most), :])
    for phase, ref in ((FEATS, fsl_s), (VALL, gv_s), (KALL, gk_s)):
        sent(phase, ref.at[pl.ds(0, span_most), :])
    for part in range(2):
        sent(SUM1 + part, dp1_s.at[part, pl.ds(0, len(lines) * half), :])
        if nz > 1:
            sent(SUM2 + part, dp2_s.at[part, pl.ds(0, (nz - 1) * half), :])
        sent(BOTH + part, wg_s.at[part, pl.ds(0, half), :])
    for copy in [ctx_copy, qg_copy, fg_copy] + out_copies:
        copy.wait()


def hand_over(*refs):
    count = len(refs) // 3
    sems = refs[-1]
    arrivals, departures = [], []
    for i in range(count):
        held = refs[2 * count + i]
        size = held.shape[0] // PIECES
        for p in range(PIECES):
            rows = pl.ds(p * size, size)
            n = i * PIECES + p
            arrivals.append(pltpu.make_async_copy(refs[i].at[rows, :], held.at[rows, :], sems.at[0, n]))
            departures.append(
                pltpu.make_async_copy(held.at[rows, :], refs[count + i].at[rows, :], sems.at[1, n])
            )
    for copy in arrivals:
        copy.start()
    for arrival, departure in zip(arrivals, departures):
        arrival.wait()
        departure.start()
    for copy in departures:
        copy.wait()


def local(ns, nd, queries, image_feats, key_weight, value_weight, image_pos, image_slot, ctx_grad):
    d, hd = key_weight.shape
    tokens, width = queries.shape[1:]
    vt = image_feats.shape[2]
    heads = width // hd
    keys = ns * vt
    chunk = GROUP_DEVICES * vt
    ds_cols = d // ns
    nx = ns // SPAN
    rows = heads * tokens

    anywhere = pl.BlockSpec(memory_space=pl.ANY)
    inside = pl.BlockSpec(memory_space=pltpu.VMEM)
    outs = pl.pallas_call(
        functools.partial(kernel, ns, nd),
        out_shape=(
            jax.ShapeDtypeStruct((tokens, width), BF16),
            jax.ShapeDtypeStruct((tokens, width), BF16),
            jax.ShapeDtypeStruct((vt, d), BF16),
            jax.ShapeDtypeStruct((ds_cols, hd), F32),
            jax.ShapeDtypeStruct((ds_cols, hd), F32),
        ),
        in_specs=[anywhere] * 4 + [inside] * 2 + [anywhere],
        out_specs=[anywhere] * 5,
        scratch_shapes=[
            pltpu.VMEM((tokens, width), BF16),
            pltpu.VMEM((tokens, width), BF16),
            pltpu.VMEM((vt, d), BF16),
            pltpu.VMEM((d, 2 * hd), BF16),
            pltpu.VMEM((vt, hd), F32),
            pltpu.VMEM((keys, 2 * hd), BF16),
            pltpu.VMEM((rows, 2 * hd), BF16),
            pltpu.VMEM((rows, 2 * hd), BF16),
            pltpu.VMEM((hd, keys), BF16),
            pltpu.VMEM((hd, keys), BF16),
            pltpu.VMEM((keys, rows), BF16),
            pltpu.VMEM((heads, 2 * hd, tokens), F32),
            pltpu.VMEM((tokens, width), BF16),
            pltpu.VMEM((tokens, width), BF16),
            pltpu.VMEM((vt, d), BF16),
            pltpu.VMEM((SPAN * vt, nx * ds_cols), BF16),
            pltpu.VMEM((keys, hd), BF16),
            pltpu.VMEM((keys, hd), BF16),
            pltpu.VMEM((keys, hd), BF16),
            pltpu.VMEM((keys, hd), BF16),
            pltpu.VMEM((SPAN * vt, hd), BF16),
            pltpu.VMEM((SPAN * vt, hd), BF16),
            pltpu.VMEM((2, nx * ds_cols, hd), BF16),
            pltpu.VMEM((2, nx * ds_cols, hd), BF16),
            pltpu.VMEM((2, nd // 2 * ds_cols // 2, hd), BF16),
            pltpu.VMEM((2, ds_cols, hd), F32),
            pltpu.SemaphoreType.DMA((14,)),
            pltpu.SemaphoreType.DMA((5,)),
            pltpu.SemaphoreType.DMA((ns // GROUP_DEVICES,)),
            pltpu.SemaphoreType.DMA((12,)),
            pltpu.SemaphoreType.DMA((12,)),
        ],
        compiler_params=pltpu.CompilerParams(
            collective_id=0, has_side_effects=True, vmem_limit_bytes=56 * 1024 * 1024
        ),
    )(
        queries[0],
        image_feats.reshape(vt, d),
        key_weight,
        value_weight,
        image_pos,
        image_slot,
        ctx_grad[0],
    )
    context, query_grad, feats_grad, key_wgrad, value_wgrad = pl.pallas_call(
        hand_over,
        out_shape=tuple(jax.ShapeDtypeStruct(out.shape, out.dtype) for out in outs),
        in_specs=[anywhere] * 5,
        out_specs=[anywhere] * 5,
        scratch_shapes=[pltpu.VMEM(out.shape, out.dtype) for out in outs]
        + [pltpu.SemaphoreType.DMA((2, 5 * PIECES))],
        compiler_params=pltpu.CompilerParams(vmem_limit_bytes=60 * 1024 * 1024),
    )(*outs)
    return (
        context[None],
        query_grad[None],
        feats_grad.reshape(1, 1, vt, d),
        key_wgrad,
        value_wgrad,
    )


def solution(mesh):
    return jax.shard_map(
        functools.partial(local, mesh.shape["seq"], mesh.shape["dp"]),
        mesh=mesh,
        in_specs=(
            P("dp", "seq", None),
            P("dp", "seq", None, None),
            P(),
            P(),
            P("dp", None),
            P("dp", None),
            P("dp", "seq", None),
        ),
        out_specs=(
            P("dp", "seq", None),
            P("dp", "seq", None),
            P("dp", "seq", None, None),
            P("seq", None),
            P("seq", None),
        ),
        check_vma=False,
    )
```

```python
import functools

import jax
import jax.numpy as jnp
from jax import lax
from jax.experimental import pallas as pl
from jax.experimental.pallas import tpu as pltpu
from jax.sharding import PartitionSpec as P

NORM_EPS = 1e-05
LOG2E = 1.4426950408889634
HIDE = -30000.0
GROUP_DEVICES = 4
SPAN = 8
PIECES = 1
KV, FEATS, VSUM, KSUM, VALL, KALL, SUM1, SUM2, BOTH = 0, 1, 2, 3, 4, 5, 6, 8, 10
BF16 = jnp.bfloat16
F32 = jnp.float32
MESH = pl.DeviceIdType.MESH
ACROSS = (((1,), (1,)), ((), ()))


def dot(a, b):
    return jnp.dot(a, b, preferred_element_type=F32)


def dot_across(a, b):
    return lax.dot_general(a, b, ACROSS, preferred_element_type=F32)


def row_factor(rows):
    return lax.rsqrt(jnp.mean(rows * rows, axis=-1, keepdims=True) + NORM_EPS)


def norm_back(rows, upstream):
    factor = row_factor(rows)
    normed = rows * factor
    return factor * (upstream - normed * jnp.mean(upstream * normed, axis=-1, keepdims=True))


def kernel(
    ns,
    nd,
    q_hbm,
    f_hbm,
    wk_hbm,
    wv_hbm,
    pos_ref,
    slot_ref,
    c_hbm,
    ctx_hbm,
    qg_hbm,
    fg_hbm,
    kw_hbm,
    vw_hbm,
    q_s,
    c_s,
    f_s,
    w_s,
    key_s,
    kv_s,
    y_s,
    do_s,
    vt_s,
    kt_s,
    e_s,
    ot_s,
    ctx_s,
    qg_s,
    fg_s,
    fsl_s,
    sendv_s,
    sendk_s,
    rsv_s,
    rsk_s,
    gv_s,
    gk_s,
    dp1_s,
    dp1r_s,
    dp2_s,
    wg_s,
    in_sem,
    out_sem,
    ag_recv,
    xs,
    xr,
):
    tokens, width = q_s.shape
    hd = 128
    heads = width // hd
    vt, d = f_s.shape
    ds_cols = d // ns
    chunk = GROUP_DEVICES * vt
    ng = ns // GROUP_DEVICES
    keys = ns * vt
    scale = hd ** (-0.5)
    half = ds_cols // 2
    nx = ns // SPAN
    nz = nd // 2

    me = lax.axis_index("seq")
    doc = lax.axis_index("dp")
    my_group = lax.div(me, GROUP_DEVICES)
    my_place = lax.rem(me, GROUP_DEVICES)
    my_x = lax.div(me, SPAN)
    my_r = lax.rem(me, SPAN)
    my_zone = lax.div(doc, 2)
    my_core = lax.rem(doc, 2)

    def peer(g, j):
        return lax.rem(my_group + g, ng) * GROUP_DEVICES + lax.rem(my_place + j, GROUP_DEVICES)

    def span_peer(j):
        return lax.rem(my_r + j, SPAN)

    def zone_peer(o):
        return {"dp": lax.rem(my_zone + o, nz) * 2 + my_core}

    other_core = {"dp": my_zone * 2 + 1 - my_core}

    def block(index, size):
        return pl.ds(pl.multiple_of(index * size, size), size)

    pairs = [(g, j) for g in range(ng) for j in range(GROUP_DEVICES) if (g, j) != (0, 0)]

    steps = 4
    depth = d // steps
    w_copies = []
    for k in range(steps):
        rows = pl.ds(k * depth, depth)
        w_copies.append(
            (
                pltpu.make_async_copy(f_hbm.at[:, rows], f_s.at[:, rows], in_sem.at[3 * k]),
                pltpu.make_async_copy(
                    wk_hbm.at[rows, :], w_s.at[rows, pl.ds(0, hd)], in_sem.at[3 * k + 1]
                ),
                pltpu.make_async_copy(
                    wv_hbm.at[rows, :], w_s.at[rows, pl.ds(hd, hd)], in_sem.at[3 * k + 2]
                ),
            )
        )
    q_copy = pltpu.make_async_copy(q_hbm, q_s, in_sem.at[3 * steps])
    c_copy = pltpu.make_async_copy(c_hbm, c_s, in_sem.at[3 * steps + 1])
    for copies in w_copies:
        for copy in copies:
            copy.start()
    q_copy.start()
    c_copy.start()

    barrier = pltpu.get_barrier_semaphore()
    lines = [(i, k) for i in range(nx) for k in range(2) if (i, k) != (0, 0)]
    columns = [(j, x) for j in range(1, SPAN) for x in range(nx)]

    def line_peer(i, k):
        return lax.rem(my_x + i, nx), lax.rem(my_core + k, 2)

    def line_device(i, k):
        x, core = line_peer(i, k)
        return {"dp": my_zone * 2 + core, "seq": x * SPAN + my_r}

    def greet(device):
        pl.semaphore_signal(barrier, inc=1, device_id=device, device_id_type=MESH)

    for o in range(1, nz):
        greet(zone_peer(o))
    for i, k in lines:
        if k:
            greet(line_device(i, k))
    for g, j in reversed(pairs):
        greet({"seq": peer(g, j)})
    greeted = ns - 1 + nx + nz - 1

    mine = block(me, vt)

    def send(phase, src, dst, target, arrival=None):
        pltpu.make_async_remote_copy(
            src_ref=src,
            dst_ref=dst,
            send_sem=xs.at[phase],
            recv_sem=xr.at[phase] if arrival is None else arrival,
            device_id=target,
            device_id_type=MESH,
        ).start()

    def take(phase, ref, arrival=None):
        pltpu.make_async_copy(ref, ref, xr.at[phase] if arrival is None else arrival).wait()

    def sent(phase, ref):
        pltpu.make_async_copy(ref, ref, xs.at[phase]).wait()

    def send_feats(some):
        for j, x in some:
            to = span_peer(j)
            send(
                FEATS,
                f_hbm.at[:, block(x * SPAN + to, ds_cols)],
                fsl_s.at[block(my_r, vt), pl.ds(x * ds_cols, ds_cols)],
                {"seq": my_x * SPAN + to},
            )

    rows_kv = jnp.zeros((vt, 2 * hd), F32)
    for k in range(steps):
        for copy in w_copies[k]:
            copy.wait()
        rows = pl.ds(k * depth, depth)
        rows_kv = rows_kv + dot(f_s[:, rows], w_s[rows, :])
    key_rows = rows_kv[:, :hd]
    key_s[...] = key_rows
    kv_s[mine, :] = jnp.concatenate(
        [(key_rows * row_factor(key_rows)).astype(BF16), rows_kv[:, hd:].astype(BF16)], axis=1
    )
    lane = lax.broadcasted_iota(jnp.int32, (tokens, hd), 1)
    tok = me * tokens + lax.broadcasted_iota(jnp.int32, (tokens, hd), 0)
    rest = hd - pos_ref.shape[1]
    positions = jnp.concatenate([pos_ref[...], jnp.zeros((1, rest), jnp.int32)], axis=1)
    slots = jnp.concatenate([slot_ref[...], jnp.full((1, rest), -1, jnp.int32)], axis=1)
    hidden = jnp.where(positions > tok, HIDE, 0.0).astype(BF16)
    q_copy.wait()
    for h in range(heads):
        raw = q_s[:, pl.ds(h * hd, hd)].astype(F32)
        rows = pl.ds(h * tokens, tokens)
        y_s[rows, pl.ds(0, hd)] = (raw * row_factor(raw)).astype(BF16)
        y_s[rows, pl.ds(hd, hd)] = hidden

    pl.semaphore_wait(barrier, greeted)
    for g, j in pairs:
        send(KV, kv_s.at[mine, :], kv_s.at[mine, :], {"seq": peer(g, j)}, ag_recv.at[g])
    send_feats(columns)
    for x in range(nx):
        cols = block(x * SPAN + my_r, ds_cols)
        fsl_s[block(my_r, vt), pl.ds(x * ds_cols, ds_cols)] = f_s[:, cols]

    def first_pass(g, first):
        group = lax.rem(my_group - g + ng, ng)
        rows = block(group, chunk)
        pair = kv_s[rows, :]
        slot_of_key = group * GROUP_DEVICES + lax.div(
            lax.broadcasted_iota(jnp.int32, (chunk, hd), 0), vt
        )
        marks = (slots == slot_of_key).astype(F32).astype(BF16)
        key_aug = jnp.concatenate([pair[:, :hd], marks], axis=1)
        value_t = pair[:, hd:].astype(F32).T.astype(BF16)
        kt_s[:, rows] = pair[:, :hd].astype(F32).T.astype(BF16)
        value_aug = jnp.concatenate([value_t, jnp.ones((hd, chunk), BF16)], axis=0)
        for h in range(heads):
            head = pl.ds(h * tokens, tokens)
            scores = dot_across(key_aug, y_s[head, :])
            weights = jnp.exp2(scores * (scale * LOG2E)).astype(BF16)
            e_s[rows, head] = weights
            part = dot(value_aug, weights)
            if first:
                ot_s[h] = part
            else:
                ot_s[h] += part

    take(KV, kv_s.at[pl.ds(0, chunk - vt), :], ag_recv.at[0])
    first_pass(0, True)

    def first_step(g, carry):
        take(KV, kv_s.at[pl.ds(0, chunk), :], ag_recv.at[g])
        first_pass(g, False)
        return carry

    lax.fori_loop(1, ng, first_step, 0)


    c_copy.wait()
    for h in range(heads):
        cols = pl.ds(h * hd, hd)
        both = ot_s[h].T
        inverse = 1.0 / both[:, hd:]
        context = both[:, :hd] * inverse
        ctx_s[:, cols] = context.astype(BF16)
        scaled = (c_s[:, cols].astype(F32) * inverse).astype(BF16)
        centre = -jnp.sum(context * scaled.astype(F32), axis=1, keepdims=True)
        high = centre.astype(BF16).astype(F32)
        low = centre - high
        extra = jnp.where(lane == 0, high, jnp.where(lane == 1, low, 0.0)).astype(BF16)
        rows = pl.ds(h * tokens, tokens)
        do_s[rows, pl.ds(0, hd)] = scaled
        do_s[rows, pl.ds(hd, hd)] = extra
    ctx_copy = pltpu.make_async_copy(ctx_s, ctx_hbm, out_sem.at[0])
    ctx_copy.start()

    def send_group(phase, src, dst, group, first):
        for j in range(first, GROUP_DEVICES):
            to = group * GROUP_DEVICES + lax.rem(my_place + j, GROUP_DEVICES)
            send(phase, src.at[block(to, vt), :], dst.at[mine, :], {"seq": to})

    def value_part(group):
        rows = block(group, chunk)
        sendv_s[rows, :] = dot(e_s[rows, :], do_s[:, pl.ds(0, hd)]).astype(BF16)

    def value_step(g, carry):
        group = lax.rem(my_group + g, ng)
        value_part(group)
        send_group(VSUM, sendv_s, rsv_s, group, 0)
        return carry

    lax.fori_loop(1, ng, value_step, 0)
    value_part(my_group)
    send_group(VSUM, sendv_s, rsv_s, my_group, 1)
    rsv_s[mine, :] = sendv_s[mine, :]

    lane_of_key = lax.broadcasted_iota(jnp.int32, (chunk, hd), 1)
    ones_two = jnp.where(lane_of_key < 2, 1.0, 0.0).astype(BF16)

    def key_part(group):
        rows = block(group, chunk)
        value_aug = jnp.concatenate([kv_s[rows, pl.ds(hd, hd)], ones_two], axis=1)
        for h in range(heads):
            head = pl.ds(h * tokens, tokens)
            part = dot_across(value_aug, do_s[head, :])
            e_s[rows, head] = (e_s[rows, head].astype(F32) * part).astype(BF16)
        sendk_s[rows, :] = (dot(e_s[rows, :], y_s[:, pl.ds(0, hd)]) * scale).astype(BF16)

    def key_step(g, carry):
        group = lax.rem(my_group + g, ng)
        key_part(group)
        send_group(KSUM, sendk_s, rsk_s, group, 0)
        return carry

    def add_up(ref, size):
        total = ref[pl.ds(0, size), :].astype(F32)
        for s in range(1, ref.shape[0] // size):
            total = total + ref[pl.ds(s * size, size), :].astype(F32)
        return total

    most = (ns - 1) * vt
    span_most = (SPAN - 1) * vt
    own = block(my_r, vt)

    def send_all(phase, ref):
        for j in range(1, SPAN):
            send(phase, ref.at[own, :], ref.at[own, :], {"seq": my_x * SPAN + span_peer(j)})

    lax.fori_loop(1, ng, key_step, 0)
    key_part(my_group)
    send_group(KSUM, sendk_s, rsk_s, my_group, 1)
    rsk_s[mine, :] = sendk_s[mine, :]

    for h in range(heads):
        cols = pl.ds(h * hd, hd)
        upstream = dot(kt_s[...], e_s[:, pl.ds(h * tokens, tokens)]).T * scale
        qg_s[:, cols] = norm_back(q_s[:, cols].astype(F32), upstream).astype(BF16)
    qg_copy = pltpu.make_async_copy(qg_s, qg_hbm, out_sem.at[1])
    qg_copy.start()

    def sum_first(part, grads):
        dp1_s[part] = dot(feats_t, grads[...]).astype(BF16)
        for i, k in lines:
            x, core = line_peer(i, k)
            send(
                SUM1 + part,
                dp1_s.at[part, block(x * 2 + core, half), :],
                dp1r_s.at[part, block(my_x * 2 + my_core, half), :],
                line_device(i, k),
            )
        slot = block(my_x * 2 + my_core, half)
        dp1r_s[part, slot, :] = dp1_s[part, slot, :]

    def sum_second(part):
        take(SUM1 + part, dp1r_s.at[part, pl.ds(0, len(lines) * half), :])
        slot = block(my_zone, half)
        dp2_s[part, slot, :] = add_up(dp1r_s.at[part], half).astype(BF16)
        for o in sorted(range(1, nz), key=lambda o: -min(o, nz - o)):
            send(SUM2 + part, dp2_s.at[part, slot, :], dp2_s.at[part, slot, :], zone_peer(o))

    def sum_third(part):
        if nz > 1:
            take(SUM2 + part, dp2_s.at[part, pl.ds(0, (nz - 1) * half), :])
        slot = block(my_core, half)
        wg_s[part, slot, :] = add_up(dp2_s.at[part], half)
        send(BOTH + part, wg_s.at[part, slot, :], wg_s.at[part, slot, :], other_core)

    def sum_last(part, out):
        take(BOTH + part, wg_s.at[part, pl.ds(0, half), :])
        copy = pltpu.make_async_copy(wg_s.at[part], out, out_sem.at[3 + part])
        copy.start()
        return copy

    take(VSUM, rsv_s.at[pl.ds(0, most), :])
    gv_s[own, :] = add_up(rsv_s, vt).astype(BF16)
    send_all(VALL, gv_s)

    take(FEATS, fsl_s.at[pl.ds(0, span_most), :])
    feats_t = fsl_s[...].astype(F32).T.astype(BF16)

    take(KSUM, rsk_s.at[pl.ds(0, most), :])
    gk_s[own, :] = norm_back(key_s[...], add_up(rsk_s, vt)).astype(BF16)
    send_all(KALL, gk_s)

    take(VALL, gv_s.at[pl.ds(0, span_most), :])
    sum_first(0, gv_s)

    row_grads = jnp.concatenate([gk_s[own, :], gv_s[own, :]], axis=1)
    for k in range(steps):
        rows = pl.ds(k * depth, depth)
        fg_s[:, rows] = dot_across(row_grads, w_s[rows, :]).astype(BF16)
    fg_copy = pltpu.make_async_copy(fg_s, fg_hbm, out_sem.at[2])
    fg_copy.start()

    take(KALL, gk_s.at[pl.ds(0, span_most), :])
    sum_first(1, gk_s)
    sum_second(0)
    sum_second(1)
    sum_third(0)
    sum_third(1)
    out_copies = [sum_last(0, vw_hbm), sum_last(1, kw_hbm)]

    for phase, ref in ((KV, kv_s), (VSUM, sendv_s), (KSUM, sendk_s)):
        sent(phase, ref.at[pl.ds(0, most), :])
    for phase, ref in ((FEATS, fsl_s), (VALL, gv_s), (KALL, gk_s)):
        sent(phase, ref.at[pl.ds(0, span_most), :])
    for part in range(2):
        sent(SUM1 + part, dp1_s.at[part, pl.ds(0, len(lines) * half), :])
        if nz > 1:
            sent(SUM2 + part, dp2_s.at[part, pl.ds(0, (nz - 1) * half), :])
        sent(BOTH + part, wg_s.at[part, pl.ds(0, half), :])
    for copy in [ctx_copy, qg_copy, fg_copy] + out_copies:
        copy.wait()


def hand_over(*refs):
    count = len(refs) // 3
    sems = refs[-1]
    arrivals, departures = [], []
    for i in range(count):
        held = refs[2 * count + i]
        size = held.shape[0] // PIECES
        for p in range(PIECES):
            rows = pl.ds(p * size, size)
            n = i * PIECES + p
            arrivals.append(pltpu.make_async_copy(refs[i].at[rows, :], held.at[rows, :], sems.at[0, n]))
            departures.append(
                pltpu.make_async_copy(held.at[rows, :], refs[count + i].at[rows, :], sems.at[1, n])
            )
    for copy in arrivals:
        copy.start()
    for arrival, departure in zip(arrivals, departures):
        arrival.wait()
        departure.start()
    for copy in departures:
        copy.wait()


def local(ns, nd, queries, image_feats, key_weight, value_weight, image_pos, image_slot, ctx_grad):
    d, hd = key_weight.shape
    tokens, width = queries.shape[1:]
    vt = image_feats.shape[2]
    heads = width // hd
    keys = ns * vt
    chunk = GROUP_DEVICES * vt
    ds_cols = d // ns
    nx = ns // SPAN
    rows = heads * tokens

    anywhere = pl.BlockSpec(memory_space=pl.ANY)
    inside = pl.BlockSpec(memory_space=pltpu.VMEM)
    outs = pl.pallas_call(
        functools.partial(kernel, ns, nd),
        out_shape=(
            jax.ShapeDtypeStruct((tokens, width), BF16),
            jax.ShapeDtypeStruct((tokens, width), BF16),
            jax.ShapeDtypeStruct((vt, d), BF16),
            jax.ShapeDtypeStruct((ds_cols, hd), F32),
            jax.ShapeDtypeStruct((ds_cols, hd), F32),
        ),
        in_specs=[anywhere] * 4 + [inside] * 2 + [anywhere],
        out_specs=[anywhere] * 5,
        scratch_shapes=[
            pltpu.VMEM((tokens, width), BF16),
            pltpu.VMEM((tokens, width), BF16),
            pltpu.VMEM((vt, d), BF16),
            pltpu.VMEM((d, 2 * hd), BF16),
            pltpu.VMEM((vt, hd), F32),
            pltpu.VMEM((keys, 2 * hd), BF16),
            pltpu.VMEM((rows, 2 * hd), BF16),
            pltpu.VMEM((rows, 2 * hd), BF16),
            pltpu.VMEM((hd, keys), BF16),
            pltpu.VMEM((hd, keys), BF16),
            pltpu.VMEM((keys, rows), BF16),
            pltpu.VMEM((heads, 2 * hd, tokens), F32),
            pltpu.VMEM((tokens, width), BF16),
            pltpu.VMEM((tokens, width), BF16),
            pltpu.VMEM((vt, d), BF16),
            pltpu.VMEM((SPAN * vt, nx * ds_cols), BF16),
            pltpu.VMEM((keys, hd), BF16),
            pltpu.VMEM((keys, hd), BF16),
            pltpu.VMEM((keys, hd), BF16),
            pltpu.VMEM((keys, hd), BF16),
            pltpu.VMEM((SPAN * vt, hd), BF16),
            pltpu.VMEM((SPAN * vt, hd), BF16),
            pltpu.VMEM((2, nx * ds_cols, hd), BF16),
            pltpu.VMEM((2, nx * ds_cols, hd), BF16),
            pltpu.VMEM((2, nd // 2 * ds_cols // 2, hd), BF16),
            pltpu.VMEM((2, ds_cols, hd), F32),
            pltpu.SemaphoreType.DMA((14,)),
            pltpu.SemaphoreType.DMA((5,)),
            pltpu.SemaphoreType.DMA((ns // GROUP_DEVICES,)),
            pltpu.SemaphoreType.DMA((12,)),
            pltpu.SemaphoreType.DMA((12,)),
        ],
        compiler_params=pltpu.CompilerParams(
            collective_id=0, has_side_effects=True, vmem_limit_bytes=56 * 1024 * 1024
        ),
    )(
        queries[0],
        image_feats.reshape(vt, d),
        key_weight,
        value_weight,
        image_pos,
        image_slot,
        ctx_grad[0],
    )
    context, query_grad, feats_grad, key_wgrad, value_wgrad = pl.pallas_call(
        hand_over,
        out_shape=tuple(jax.ShapeDtypeStruct(out.shape, out.dtype) for out in outs),
        in_specs=[anywhere] * 5,
        out_specs=[anywhere] * 5,
        scratch_shapes=[pltpu.VMEM(out.shape, out.dtype) for out in outs]
        + [pltpu.SemaphoreType.DMA((2, 5 * PIECES))],
        compiler_params=pltpu.CompilerParams(vmem_limit_bytes=60 * 1024 * 1024),
    )(*outs)
    return (
        context[None],
        query_grad[None],
        feats_grad.reshape(1, 1, vt, d),
        key_wgrad,
        value_wgrad,
    )


def solution(mesh):
    return jax.shard_map(
        functools.partial(local, mesh.shape["seq"], mesh.shape["dp"]),
        mesh=mesh,
        in_specs=(
            P("dp", "seq", None),
            P("dp", "seq", None, None),
            P(),
            P(),
            P("dp", None),
            P("dp", None),
            P("dp", "seq", None),
        ),
        out_specs=(
            P("dp", "seq", None),
            P("dp", "seq", None),
            P("dp", "seq", None, None),
            P("seq", None),
            P("seq", None),
        ),
        check_vma=False,
    )
```
